32 devices in a mesh: leaf: 8 (over z, x), col: 4 (over y, core).
Axes of the slice: x: 2, y: 2, z: 4, core: 2. Of those that a mesh axis runs over, the one named last changes fastest.
Arguments:
- points: float32 [8192, 128], P(('leaf', 'col')), may hold values from -6 to 6
- coefs: float32 [8192, 512], P(('leaf', 'col')), may hold values from -6 to 6
- targets: float32 [8192, 512], P(('leaf', 'col')), may hold values from -6 to 6
- ridge: float32 [1], replicated, may hold values from 0.5 to 2
- tile_mask: int32 [8, 5], P('leaf'), may hold values from 0 to 1, as said below
- cluster_perm: int32 [8, 1024], P('leaf'), may hold values from 0 to 1023, each once within a row
- leaf_map: int32 [8], replicated, may hold values from 0 to 7, as said below
- leaf_inverse: float32 [8, 1024, 1024], P('leaf'), may hold values from -0.25 to 1.3
- leaf_basis: float32 [8, 1024, 256], P('leaf'), may hold values from -0.1875 to 0.1875
- node_inverse: float32 [8, 320, 1024], P('leaf'), may hold values from -0.25 to 1.3
- node_transfer: float32 [8, 320, 256], P('leaf'), may hold values from -0.1875 to 0.1875
Outputs:
- residual: float32 [8192, 512], P(('leaf', 'col'))
- new_coef: float32 [8192, 512], P(('leaf', 'col'))
The draws below stay inside these ranges and needn't reach their ends.
Inputs may be any that keep to these rules, and one draw needn't show every extreme that they name: `tile_mask`: entry k of row i is 1 when block i has a nonzero tile with block i + k - 2; entry 2 is always 1, entries naming a block outside 0 .. 7 are 0, and some row lists all 5 tiles. `cluster_perm`: each row is a permutation of 0 .. 1023. `leaf_map`: a permutation of 0 .. 7 that sends the tree leaves 4 n .. 4 n + 3 to the blocks 4 n .. 4 n + 3.
All inputs are finite; a program needn't handle non-finite values.
Results may differ from the reference program's by a relative error of at most 0.0003.
Values sent between devices are 32-bit elements; how exact they have to be, the bound alone decides.
A program may use at most 128 MiB of HBM per device.

```python
import math
import jax
import jax.numpy as jnp
from jax import lax

F = 128
R = 512
LEAF = 1024
RANK = 256
WIN = 2
LEAVES = 8
NPTS = 8192
SLICE_ROWS = 320


def slice_layout(remaining, rank_size):
    layout = []
    covered = 1
    while remaining > 1:
        children = 4 if remaining % 4 == 0 else remaining
        covered = covered * children
        remaining = remaining // children
        layout.append((covered, children * rank_size // covered))
    return layout


def diagonal_heavy(key, count, order_size):
    first_key, second_key = jax.random.split(key)
    identity = jnp.eye(order_size, dtype=jnp.float32)
    diagonal = jax.random.uniform(first_key, (count, order_size), jnp.float32, 0.6, 1.2)
    spread = jnp.clip(jax.random.normal(second_key, (count, order_size, order_size), jnp.float32), -4.0, 4.0)
    scaled = spread * (0.3 * order_size ** (-0.5))
    return scaled * (1.0 - identity) + diagonal[:, :, None] * identity


def draw_leaf_inverse(key, part):
    return diagonal_heavy(jax.random.fold_in(key, 11), LEAVES, LEAF)


def draw_node_inverse(key, part):
    first_key, second_key = jax.random.split(jax.random.fold_in(key, 23))
    order_size = 4 * RANK
    targets_list = []
    for covered, slice_count in slice_layout(LEAVES, RANK):
        device = jnp.arange(LEAVES, dtype=jnp.int32)[:, None]
        local = jnp.arange(slice_count, dtype=jnp.int32)[None, :]
        targets_list.append(device % covered * slice_count + local)
    target = jnp.concatenate(targets_list, axis=1)
    slice_total = target.shape[1]
    diagonal = jax.random.uniform(first_key, (LEAVES, slice_total), jnp.float32, 0.6, 1.2)
    spread = jnp.clip(jax.random.normal(second_key, (LEAVES, slice_total, order_size), jnp.float32), -4.0, 4.0)
    columns = jnp.arange(order_size, dtype=jnp.int32)[None, None, :]
    on_diagonal = columns == target[:, :, None]
    return jnp.where(on_diagonal, diagonal[:, :, None], spread * (0.3 * order_size ** (-0.5)))


def draw_tile_mask(key, part):
    first_key, second_key, third_key = jax.random.split(jax.random.fold_in(key, 5), 3)
    density = jax.random.randint(first_key, (LEAVES, 1), 1, 5)
    coins = jax.random.randint(second_key, (LEAVES, 2 * WIN + 1), 0, 4)
    full_row = jax.random.randint(third_key, (), WIN, LEAVES - WIN)
    rows = jnp.arange(LEAVES, dtype=jnp.int32)[:, None]
    slots = jnp.arange(2 * WIN + 1, dtype=jnp.int32)[None, :]
    target_block = rows + slots - WIN
    inside = (target_block >= 0) & (target_block < LEAVES)
    chosen = (coins < density) | (slots == WIN) | (rows == full_row)
    return (chosen & inside).astype(jnp.int32)


def draw_leaf_map(key, part):
    group_keys = jax.random.split(jax.random.fold_in(key, 7), LEAVES // 4)
    shuffles = jax.vmap(lambda group_key: jax.random.permutation(group_key, 4).astype(jnp.int32))(group_keys)
    offsets = 4 * jnp.arange(LEAVES // 4, dtype=jnp.int32)[:, None]
    return (shuffles + offsets).reshape(LEAVES).astype(jnp.int32)


def level_of(stream_key, dims, cuts, smallest, top_value):
    loudness, own = 1.0, jax.random.fold_in(stream_key, 6)
    for axis_at, shards_of in cuts:
        draws = jnp.exp(jax.random.uniform(jax.random.fold_in(own, axis_at), (shards_of,), jnp.float32, smallest / len(cuts), top_value / len(cuts)))
        loudness = loudness * jnp.repeat(draws, dims[axis_at] // shards_of).reshape([-1 if axis == axis_at else 1 for axis in range(len(dims))])
    return loudness


def scatter_about(own_key, extent, width, bound, shards=(), held_as=jnp.bfloat16):
    array = width * jax.random.normal(own_key, extent, jnp.float32)
    if shards:
        array = array * level_of(own_key, extent, shards, -0.22, 0.18)
    return jnp.clip(array, -bound, bound).astype(held_as)


def setup_inputs(seed: int = 0) -> dict:
    streams_of = jax.random.split(jax.random.key(seed), 12)
    points = scatter_about(streams_of[0], (NPTS, F), 1.0, 6.0, ((0, 32),), jnp.float32)
    coefs = scatter_about(streams_of[1], (NPTS, R), 1.0, 6.0, ((0, 32),), jnp.float32)
    targets = scatter_about(streams_of[2], (NPTS, R), 1.0, 6.0, ((0, 32),), jnp.float32)
    ridge = jnp.clip(jnp.exp(jax.random.uniform(streams_of[3], (1,), jnp.float32, math.log(0.5), math.log(2.0))), 0.5, 2.0)
    tile_mask = draw_tile_mask(jax.random.fold_in(streams_of[11], 71), 0)
    cluster_perm = jax.vmap(lambda own: jax.random.permutation(own, LEAF))(jax.random.split(streams_of[5], LEAVES)).reshape((LEAVES, LEAF)).astype(jnp.int32)
    leaf_map = draw_leaf_map(jax.random.fold_in(streams_of[11], 71), 0)
    leaf_inverse = draw_leaf_inverse(jax.random.fold_in(streams_of[11], 71), 0)
    leaf_basis = scatter_about(streams_of[8], (LEAVES, LEAF, RANK), (4 * RANK) ** -0.5, 0.1875, ((0, 8),), jnp.float32)
    node_inverse = draw_node_inverse(jax.random.fold_in(streams_of[11], 71), 0)
    node_transfer = scatter_about(streams_of[10], (LEAVES, SLICE_ROWS, RANK), (4 * RANK) ** -0.5, 0.1875, ((0, 8),), jnp.float32)
    return {"points": points, "coefs": coefs, "targets": targets, "ridge": ridge, "tile_mask": tile_mask, "cluster_perm": cluster_perm, "leaf_map": leaf_map, "leaf_inverse": leaf_inverse, "leaf_basis": leaf_basis, "node_inverse": node_inverse, "node_transfer": node_transfer}


highest = lax.Precision.HIGHEST


def kernel_tile(row_points, row_squares, column_points, column_squares):
    inner_products = jnp.einsum("pf,qf->pq", row_points, column_points, precision=highest)
    distance = row_squares[:, None] + column_squares[None, :] - 2.0 * inner_products
    return jnp.exp(distance * (-2.0 / row_points.shape[1]))


def tree_levels(remaining, rank_size):
    levels = []
    covered = 1
    height = 1
    offset = 0
    while remaining > 1:
        children = 4 if remaining % 4 == 0 else remaining
        covered = covered * children
        remaining = remaining // children
        slice_count = children * rank_size // covered
        levels.append((height, children, covered, offset, slice_count))
        offset = offset + slice_count
        height = height + 1
    return levels


def reference(points, coefs, targets, ridge, tile_mask, cluster_perm, leaf_map, leaf_inverse, leaf_basis, node_inverse, node_transfer):
    perm_index = cluster_perm[:, :, None]
    ordered_x = jnp.take_along_axis(points.reshape(LEAVES, LEAF, F), perm_index, axis=1)
    ordered_a = jnp.take_along_axis(coefs.reshape(LEAVES, LEAF, R), perm_index, axis=1)
    ordered_y = jnp.take_along_axis(targets.reshape(LEAVES, LEAF, R), perm_index, axis=1)
    squares = jnp.sum(ordered_x * ordered_x, axis=2)

    def block_residual(block):
        tile_total = jnp.zeros((LEAF, R), jnp.float32)
        for band_slot in range(2 * WIN + 1):
            other = jnp.clip(block + band_slot - WIN, 0, LEAVES - 1).astype(jnp.int32)
            kernel = kernel_tile(ordered_x[block], squares[block], ordered_x[other], squares[other])
            term = jnp.dot(kernel, ordered_a[other], precision=highest)
            tile_total = tile_total + jnp.where(tile_mask[block, band_slot] > 0, term, jnp.zeros_like(term))
        return ordered_y[block] - ridge[0] * ordered_a[block] - tile_total

    residual_c = lax.map(block_residual, jnp.arange(LEAVES, dtype=jnp.int32))
    solved = jnp.einsum("bpq,bqc->bpc", leaf_inverse, residual_c, precision=highest)
    reduced = jnp.einsum("bpr,bpc->brc", leaf_basis, solved, precision=highest)
    current = reduced[leaf_map]
    stored = []
    slice_total = node_inverse.shape[1]
    levels = tree_levels(LEAVES, RANK)
    for height, children, covered, offset, slice_count in levels:
        node_count = current.shape[0] // children
        node_rows = children * RANK
        stacked = current.reshape(node_count, node_rows, R)
        node_inv = node_inverse.reshape(node_count, covered, slice_total, 4 * RANK)[:, :, offset:offset + slice_count, :node_rows].reshape(node_count, node_rows, node_rows)
        transfer_rows = node_transfer.reshape(node_count, covered, slice_total, RANK)[:, :, offset:offset + slice_count, :].reshape(node_count, node_rows, RANK)
        weights = jnp.einsum("nab,nbc->nac", node_inv, stacked, precision=highest)
        stored.append((weights, node_inv, transfer_rows))
        current = jnp.einsum("nar,nac->nrc", transfer_rows, weights, precision=highest)
    values = stored[-1][0]
    for position in range(len(levels) - 2, -1, -1):
        weights, node_inv, transfer_rows = stored[position]
        pieces = values.reshape(weights.shape[0], RANK, R)
        lifted = jnp.einsum("nar,nrc->nac", transfer_rows, pieces, precision=highest)
        values = weights - jnp.einsum("nab,nbc->nac", node_inv, lifted, precision=highest)
    leaf_pieces = values.reshape(LEAVES, RANK, R)
    inverse_map = jnp.zeros((LEAVES,), jnp.int32).at[leaf_map].set(jnp.arange(LEAVES, dtype=jnp.int32))
    pieces = leaf_pieces[inverse_map]
    lifted = jnp.einsum("bpr,brc->bpc", leaf_basis, pieces, precision=highest)
    correction = jnp.einsum("bpq,bqc->bpc", leaf_inverse, lifted, precision=highest)
    fresh = ordered_a + (solved - correction)

    def invert_row(row_perm):
        return jnp.zeros((LEAF,), jnp.int32).at[row_perm].set(jnp.arange(LEAF, dtype=jnp.int32))

    back_index = jax.vmap(invert_row)(cluster_perm)[:, :, None]
    residual = jnp.take_along_axis(residual_c, back_index, axis=1).reshape(NPTS, R)
    new_coef = jnp.take_along_axis(fresh, back_index, axis=1).reshape(NPTS, R)
    return residual, new_coef
```

```python
import jax
import jax.numpy as jnp
from jax import lax
from jax.sharding import PartitionSpec as P

high = lax.Precision.HIGH


def swap_route(count, mask):
    return [(place, place ^ mask) for place in range(count)]


def partner_of(block, axis, mask):
    return lax.ppermute(block, axis, swap_route(lax.axis_size(axis), mask))


def shifted(value, axis, steps):
    count = lax.axis_size(axis)
    initial, last = (max(0, -steps), min(count, count - steps))
    return lax.ppermute(value, axis, [(source, source + steps) for source in range(initial, last)])


def exchange_raw(block, axis, low, fan):
    return [block] + [partner_of(block, axis, m << low) for m in range(1, fan)]


def in_order(pieces, digit):
    pieces = list(pieces)
    bit = 0
    while 1 << bit < len(pieces):
        odd = (digit >> bit) % 2 == 1
        pieces = [jnp.where(odd, pieces[m ^ (1 << bit)], pieces[m]) for m in range(len(pieces))]
        bit += 1
    return pieces


def exchange(block, axis, pos, low, fan):
    return in_order(exchange_raw(block, axis, low, fan), (pos >> low) % fan)


def tree_levels(remaining, rank_size):
    levels = []
    covered = 1
    offset = 0
    while remaining > 1:
        children = 4 if remaining % 4 == 0 else remaining
        low = covered.bit_length() - 1
        covered = covered * children
        remaining = remaining // children
        slice_count = children * rank_size // covered
        levels.append((children, low, offset, slice_count))
        offset = offset + slice_count
    return levels


def mm(a, b):
    return jnp.dot(a, b, precision=high)


def mm_t(a, b):
    return jnp.einsum("ka,kc->ac", a, b, precision=high)


def to_rows(block, col_pos, col_count):
    share = block.shape[0] // col_count
    width = block.shape[1]
    out = jnp.zeros((share, width * col_count), block.dtype)
    for m in range(col_count):
        target = col_pos ^ m
        piece = lax.dynamic_slice_in_dim(block, target * share, share, 0)
        if m:
            piece = partner_of(piece, "col", m)
        out = lax.dynamic_update_slice(out, piece, (0, target * width))
    return out


def local(
    points,
    coefs,
    targets,
    ridge,
    tile_mask,
    cluster_perm,
    leaf_map,
    leaf_inverse,
    leaf_basis,
    node_inverse,
    node_transfer,
):
    col_count = lax.axis_size("col")
    col_pos = lax.axis_index("col")
    leaf_count = lax.axis_size("leaf")
    leaf_pos = lax.axis_index("leaf")
    share_rows, features = points.shape
    leaf_size = share_rows * col_count
    target_width = coefs.shape[1]
    col_width = target_width // col_count
    band_reach = tile_mask.shape[1] // 2
    scale = -2.0 / features

    packed = jnp.concatenate([points, coefs], axis=1)
    fetched = {0: packed}
    for offset in range(-band_reach, band_reach + 1):
        if offset != 0:
            fetched[offset] = shifted(packed, "leaf", -offset)
    rows_x = lax.all_gather(points, "col", axis=0, tiled=True)
    row_squares = jnp.sum(rows_x * rows_x, axis=1)

    def kernel_of(offset):
        column_points = fetched[offset][:, :features]
        squares = jnp.sum(column_points * column_points, axis=1)
        inner = jnp.einsum("pf,qf->pq", rows_x, column_points, precision=high)
        values = jnp.exp((row_squares[:, None] + squares[None, :] - 2.0 * inner) * scale)
        return jnp.where(tile_mask[0, offset + band_reach] > 0, values, 0.0)

    basis = leaf_basis[0]
    solve = leaf_inverse[0]
    rank_size = basis.shape[1]
    order = cluster_perm[0]
    spread = (order[:, None] == jnp.arange(leaf_size, dtype=jnp.int32)[None, :]).astype(jnp.float32)
    down_map = mm_t(spread, mm(solve, basis))
    up_map = mm(mm_t(basis, solve), spread)

    levels = tree_levels(leaf_count, rank_size)
    share_rank = rank_size // col_count
    shared = []
    for number, (children, low, offset, slice_count) in enumerate(levels):
        node_rows = children * rank_size
        node_inv = node_inverse[0, offset : offset + slice_count, :node_rows]
        if number > 0:
            part = slice_count // col_count
            mine = lax.dynamic_slice_in_dim(node_inv, col_pos * part, part, 0)[None]
            for below in range(number):
                fan, below_low = levels[below][:2]
                mine = jnp.concatenate(exchange(mine, "leaf", leaf_pos, below_low, fan), axis=0)
            every = lax.all_gather(mine, "col", axis=1, tiled=True)
            own_inv = every.reshape(rank_size, node_rows)
        else:
            own_inv = node_inv
        lift = None
        merge = None
        if number < len(levels) - 1:
            transfer = lax.dynamic_slice(
                node_transfer[0], (offset, col_pos * share_rank), (slice_count, share_rank)
            ).T
            part_merge = mm(transfer, node_inv)
            whole = transfer
            for fan, digit_low in [level[:2] for level in levels[: number + 1]]:
                whole = jnp.concatenate(exchange(whole, "leaf", leaf_pos, digit_low, fan), axis=1)
                for bit in range(fan.bit_length() - 1):
                    part_merge = part_merge + partner_of(part_merge, "leaf", 1 << (digit_low + bit))
            part_lift = jnp.einsum("ra,ba->rb", whole, own_inv, precision=high)
            both = lax.all_gather(
                jnp.concatenate([part_merge, part_lift], axis=1), "col", axis=0, tiled=True
            )
            merge = both[:, :node_rows]
            lift = both[:, node_rows:]
        shared.append((own_inv, merge, lift))

    base = targets - ridge[0] * coefs
    base_rows = lax.dynamic_update_slice(
        jnp.zeros((leaf_size, target_width), jnp.float32), base, (col_pos * share_rows, 0)
    )
    groups = [[0]]
    for reach in range(1, band_reach + 1):
        groups.append([-reach, reach])
    partial = base_rows
    for group in groups:
        kernel = jnp.concatenate([kernel_of(offset) for offset in group], axis=1)
        group_coefs = jnp.concatenate([fetched[offset][:, features:] for offset in group], axis=0)
        partial = partial - mm(kernel, group_coefs)
    bit = 0
    pieces = partial.reshape(leaf_size, target_width)
    while 1 << bit < col_count:
        width = col_width << bit
        view = pieces.reshape(leaf_size, -1, 2, col_width)
        side = (col_pos >> bit) % 2
        keep = lax.dynamic_slice_in_dim(view, side, 1, 2).reshape(leaf_size, -1)
        give = lax.dynamic_slice_in_dim(view, 1 - side, 1, 2).reshape(leaf_size, -1)
        pieces = keep + partner_of(give, "col", 1 << bit)
        bit += 1
    residual = pieces

    current = mm(up_map, residual)
    stacks = []
    for number, (children, low, offset, slice_count) in enumerate(levels):
        ordered = exchange(current, "leaf", leaf_pos, low, children)
        if number == 0:
            group_base = leaf_pos // children * children
            slots = lax.dynamic_slice_in_dim(leaf_map, group_base, children, 0) - group_base
            picked = []
            for slot in range(children):
                piece = ordered[0]
                for source in range(1, children):
                    piece = jnp.where(slots[slot] == source, ordered[source], piece)
                picked.append(piece)
            ordered = picked
        stacked = jnp.concatenate(ordered, axis=0)
        stacks.append(stacked)
        if number < len(levels) - 1:
            current = mm(shared[number][1], stacked)
    values = None
    for number in range(len(levels) - 1, -1, -1):
        own_inv, merge, lift = shared[number]
        fresh_values = mm(own_inv, stacks[number])
        values = fresh_values if values is None else fresh_values - mm_t(lift, values)
    children = levels[0][0]
    local_index = leaf_pos % children
    raw = exchange_raw(values, "leaf", 0, children)
    own_slot = jnp.sum(jnp.arange(children, dtype=jnp.int32) * (slots == local_index))
    incoming = raw[0]
    for m in range(1, children):
        incoming = jnp.where(own_slot == local_index ^ m, raw[m], incoming)

    residual_rows = to_rows(residual, col_pos, col_count)
    solved = mm_t(spread, mm(solve, mm(spread, residual)))
    step = solved - mm(down_map, incoming)
    fresh_rows = coefs + to_rows(step, col_pos, col_count)
    return (residual_rows, fresh_rows)


def solution(mesh):
    return jax.shard_map(
        local,
        mesh=mesh,
        in_specs=(
            P(("leaf", "col"), None),
            P(("leaf", "col"), None),
            P(("leaf", "col"), None),
            P(),
            P("leaf", None),
            P("leaf", None),
            P(),
            P("leaf", None, None),
            P("leaf", None, None),
            P("leaf", None, None),
            P("leaf", None, None),
        ),
        out_specs=(P(("leaf", "col"), None), P(("leaf", "col"), None)),
        check_vma=False,
    )
```

```python
import functools

import jax
import jax.numpy as jnp
from jax import lax
from jax.experimental import pallas as pl
from jax.experimental.pallas import tpu as pltpu
from jax.sharding import PartitionSpec as P

high = lax.Precision.HIGH


def swap_route(count, mask):
    return [(place, place ^ mask) for place in range(count)]


def partner_of(block, axis, mask):
    return lax.ppermute(block, axis, swap_route(lax.axis_size(axis), mask))


def shifted(value, axis, steps):
    count = lax.axis_size(axis)
    initial, last = (max(0, -steps), min(count, count - steps))
    return lax.ppermute(value, axis, [(source, source + steps) for source in range(initial, last)])


def exchange_raw(block, axis, low, fan):
    return [block] + [partner_of(block, axis, m << low) for m in range(1, fan)]


def in_order(pieces, digit):
    pieces = list(pieces)
    bit = 0
    while 1 << bit < len(pieces):
        odd = (digit >> bit) % 2 == 1
        pieces = [jnp.where(odd, pieces[m ^ (1 << bit)], pieces[m]) for m in range(len(pieces))]
        bit += 1
    return pieces


def exchange(block, axis, pos, low, fan):
    return in_order(exchange_raw(block, axis, low, fan), (pos >> low) % fan)


def tree_levels(remaining, rank_size):
    levels = []
    covered = 1
    offset = 0
    while remaining > 1:
        children = 4 if remaining % 4 == 0 else remaining
        low = covered.bit_length() - 1
        covered = covered * children
        remaining = remaining // children
        slice_count = children * rank_size // covered
        levels.append((children, low, offset, slice_count))
        offset = offset + slice_count
    return levels


def mm(a, b):
    return jnp.dot(a, b, precision=high)


def mm_t(a, b):
    return jnp.einsum("ka,kc->ac", a, b, precision=high)


def to_rows(block, col_pos, col_count):
    share = block.shape[0] // col_count
    width = block.shape[1]
    out = jnp.zeros((share, width * col_count), block.dtype)
    for m in range(col_count):
        target = col_pos ^ m
        piece = lax.dynamic_slice_in_dim(block, target * share, share, 0)
        if m:
            piece = partner_of(piece, "col", m)
        out = lax.dynamic_update_slice(out, piece, (0, target * width))
    return out


def halves(value):
    top = value.astype(jnp.bfloat16)
    return top, (value - top.astype(jnp.float32)).astype(jnp.bfloat16)


def product(left, right, contract):
    def one(a, b):
        return lax.dot_general(a, b, (contract, ((), ())), preferred_element_type=jnp.float32)

    return one(left[0], right[0]) + (one(left[0], right[1]) + one(left[1], right[0]))


def band_body(count, features, cols, *refs):
    mask_ref, ridge_ref, pos_ref, rows_ref, targets_ref = refs[:5]
    fetched = refs[5 : 5 + count]
    outs = refs[5 + count : 5 + count + cols]
    x_top, x_low, a_top, a_low, squares = refs[5 + count + cols :]
    step = pl.program_id(0)
    share = targets_ref.shape[0]
    flat = ((1,), (1,))

    @pl.when(step == 0)
    def _():
        ones = jnp.ones((8, features), jnp.bfloat16)
        for k in range(count):
            span = pl.ds(k * share, share)
            x = fetched[k][:, :features]
            x_top[span, :], x_low[span, :] = halves(x)
            a_top[span, :], a_low[span, :] = halves(fetched[k][:, features:])
            first, rest = halves(x * x)
            last = (x * x - first.astype(jnp.float32) - rest.astype(jnp.float32)).astype(
                jnp.bfloat16
            )
            total = jnp.zeros((8, share), jnp.float32)
            for part in (last, rest, first):
                total += lax.dot_general(
                    ones, part, (flat, ((), ())), preferred_element_type=jnp.float32
                )
            squares[:, span] = total

    rows = rows_ref[...]
    row_squares = jnp.sum(rows * rows, axis=1, keepdims=True)
    row_halves = halves(rows)
    own = fetched[count // 2][:, features:]
    base = targets_ref[...] - ridge_ref[0] * own
    total = jnp.where(step == pos_ref[0], base, jnp.zeros_like(base))
    for k in range(count):
        span = pl.ds(k * share, share)
        inner = product(row_halves, (x_top[span, :], x_low[span, :]), flat)
        distance = row_squares + squares[0:1, span] - 2.0 * inner
        kernel = jnp.exp(distance * (-2.0 / features))
        kernel = jnp.where(mask_ref[0, k] > 0, kernel, jnp.zeros_like(kernel))
        total -= product(halves(kernel), (a_top[span, :], a_low[span, :]), ((1,), (0,)))
    width = total.shape[1] // cols
    pieces = [total[:, m * width : (m + 1) * width] for m in range(cols)]
    bit = 0
    while 1 << bit < cols:
        odd = (pos_ref[0] >> bit) % 2 == 1
        pieces = [jnp.where(odd, pieces[m ^ (1 << bit)], pieces[m]) for m in range(cols)]
        bit += 1
    for out, piece in zip(outs, pieces):
        out[...] = piece


def band_products(rows_x, fetched, targets, ridge, tile_mask, col_pos, cols):
    leaf_size, features = rows_x.shape
    share, wide = fetched[0].shape
    target_width = targets.shape[1]
    width = target_width // cols
    count = len(fetched)
    smem = pl.BlockSpec(memory_space=pltpu.SMEM)
    whole = lambda shape: pl.BlockSpec(shape, lambda i: (0, 0))
    return pl.pallas_call(
        functools.partial(band_body, count, features, cols),
        grid=(leaf_size // share,),
        in_specs=[smem, smem, smem, pl.BlockSpec((share, features), lambda i: (i, 0))]
        + [whole((share, target_width))]
        + [whole((share, wide))] * count,
        out_specs=[pl.BlockSpec((share, width), lambda i: (i, 0))] * cols,
        out_shape=[jax.ShapeDtypeStruct((leaf_size, width), jnp.float32)] * cols,
        scratch_shapes=[
            pltpu.VMEM((count * share, features), jnp.bfloat16),
            pltpu.VMEM((count * share, features), jnp.bfloat16),
            pltpu.VMEM((count * share, target_width), jnp.bfloat16),
            pltpu.VMEM((count * share, target_width), jnp.bfloat16),
            pltpu.VMEM((8, count * share), jnp.float32),
        ],
        compiler_params=pltpu.CompilerParams(vmem_limit_bytes=40 * 1024 * 1024),
        cost_estimate=pl.CostEstimate(
            flops=12 * leaf_size * share * count * wide // 2,
            bytes_accessed=8 * leaf_size * target_width,
            transcendentals=leaf_size * share * count,
        ),
    )(tile_mask, ridge, jnp.reshape(col_pos, (1,)).astype(jnp.int32), rows_x, targets, *fetched)


def local(
    points,
    coefs,
    targets,
    ridge,
    tile_mask,
    cluster_perm,
    leaf_map,
    leaf_inverse,
    leaf_basis,
    node_inverse,
    node_transfer,
):
    col_count = lax.axis_size("col")
    col_pos = lax.axis_index("col")
    leaf_count = lax.axis_size("leaf")
    leaf_pos = lax.axis_index("leaf")
    share_rows, features = points.shape
    leaf_size = share_rows * col_count
    target_width = coefs.shape[1]
    col_width = target_width // col_count
    band_reach = tile_mask.shape[1] // 2

    packed = jnp.concatenate([points, coefs], axis=1)
    fetched = []
    for offset in range(-band_reach, band_reach + 1):
        fetched.append(shifted(packed, "leaf", -offset) if offset else packed)
    rows_x = lax.all_gather(points, "col", axis=0, tiled=True)

    basis = leaf_basis[0]
    solve = leaf_inverse[0]
    rank_size = basis.shape[1]
    order = cluster_perm[0]
    spread = (order[:, None] == jnp.arange(leaf_size, dtype=jnp.int32)[None, :]).astype(jnp.float32)
    up_map = mm(mm_t(basis, solve), spread)

    levels = tree_levels(leaf_count, rank_size)
    shared = []
    for number, (children, low, offset, slice_count) in enumerate(levels):
        node_rows = children * rank_size
        node_inv = node_inverse[0, offset : offset + slice_count, :node_rows]
        own_inv = node_inv
        for fan, digit_low in [level[:2] for level in levels[:number]]:
            own_inv = jnp.concatenate(exchange(own_inv, "leaf", leaf_pos, digit_low, fan), axis=0)
        transfer = None
        lift = None
        if number < len(levels) - 1:
            transfer = node_transfer[0, offset : offset + slice_count]
            whole = transfer
            for fan, digit_low in [level[:2] for level in levels[: number + 1]]:
                whole = jnp.concatenate(exchange(whole, "leaf", leaf_pos, digit_low, fan), axis=0)
            lift = mm(own_inv, whole)
        shared.append((node_inv, own_inv, transfer, lift))

    blocks = list(
        band_products(rows_x, fetched, targets, ridge, tile_mask, col_pos, col_count)
    )
    ready = blocks[-1]
    mask = 1
    while mask < col_count:
        for m in range(col_count - 2 * mask, -1, -2 * mask):
            blocks[m] = blocks[m] + partner_of(blocks[m + mask], "col", mask)
        mask *= 2
    residual = blocks[0]
    late_solve, late_basis, _ = lax.optimization_barrier((solve, basis, ready))
    down_map = mm_t(spread, mm(late_solve, late_basis))

    current = mm(up_map, residual)
    stacks = []
    for number, (children, low, offset, slice_count) in enumerate(levels):
        ordered = exchange(current, "leaf", leaf_pos, low, children)
        if number == 0:
            group_base = leaf_pos // children * children
            slots = lax.dynamic_slice_in_dim(leaf_map, group_base, children, 0) - group_base
            picked = []
            for slot in range(children):
                piece = ordered[0]
                for source in range(1, children):
                    piece = jnp.where(slots[slot] == source, ordered[source], piece)
                picked.append(piece)
            ordered = picked
        stacked = jnp.concatenate(ordered, axis=0)
        stacks.append(stacked)
        if number < len(levels) - 1:
            current = mm_t(shared[number][2], mm(shared[number][0], stacked))
            for fan, digit_low in [level[:2] for level in levels[: number + 1]]:
                current = sum(exchange_raw(current, "leaf", digit_low, fan))
    values = None
    for number in range(len(levels) - 1, -1, -1):
        node_inv, own_inv, transfer, lift = shared[number]
        fresh_values = mm(own_inv, stacks[number])
        values = fresh_values if values is None else fresh_values - mm(lift, values)
    children = levels[0][0]
    local_index = leaf_pos % children
    raw = exchange_raw(values, "leaf", 0, children)
    own_slot = jnp.sum(jnp.arange(children, dtype=jnp.int32) * (slots == local_index))
    incoming = raw[0]
    for m in range(1, children):
        incoming = jnp.where(own_slot == local_index ^ m, raw[m], incoming)

    residual_rows = to_rows(residual, col_pos, col_count)
    solved = mm_t(spread, mm(solve, mm(spread, residual)))
    step = solved - mm(down_map, incoming)
    fresh_rows = coefs + to_rows(step, col_pos, col_count)
    return (residual_rows, fresh_rows)


def solution(mesh):
    return jax.shard_map(
        local,
        mesh=mesh,
        in_specs=(
            P(("leaf", "col"), None),
            P(("leaf", "col"), None),
            P(("leaf", "col"), None),
            P(),
            P("leaf", None),
            P("leaf", None),
            P(),
            P("leaf", None, None),
            P("leaf", None, None),
            P("leaf", None, None),
            P("leaf", None, None),
        ),
        out_specs=(P(("leaf", "col"), None), P(("leaf", "col"), None)),
        check_vma=False,
    )
```

```python
import functools

import jax
import jax.numpy as jnp
from jax import lax
from jax.experimental import pallas as pl
from jax.experimental.pallas import tpu as pltpu
from jax.sharding import PartitionSpec as P

high = lax.Precision.HIGH


def swap_route(count, mask):
    return [(place, place ^ mask) for place in range(count)]


def partner_of(block, axis, mask):
    return lax.ppermute(block, axis, swap_route(lax.axis_size(axis), mask))


def shifted(value, axis, steps):
    count = lax.axis_size(axis)
    initial, last = (max(0, -steps), min(count, count - steps))
    return lax.ppermute(value, axis, [(source, source + steps) for source in range(initial, last)])


def exchange_raw(block, axis, low, fan):
    return [block] + [partner_of(block, axis, m << low) for m in range(1, fan)]


def in_order(pieces, digit):
    pieces = list(pieces)
    bit = 0
    while 1 << bit < len(pieces):
        odd = (digit >> bit) % 2 == 1
        pieces = [jnp.where(odd, pieces[m ^ (1 << bit)], pieces[m]) for m in range(len(pieces))]
        bit += 1
    return pieces


def exchange(block, axis, pos, low, fan):
    return in_order(exchange_raw(block, axis, low, fan), (pos >> low) % fan)


def tree_levels(remaining, rank_size):
    levels = []
    covered = 1
    offset = 0
    while remaining > 1:
        children = 4 if remaining % 4 == 0 else remaining
        low = covered.bit_length() - 1
        covered = covered * children
        remaining = remaining // children
        slice_count = children * rank_size // covered
        levels.append((children, low, offset, slice_count))
        offset = offset + slice_count
    return levels


def mm(a, b):
    return jnp.dot(a, b, precision=high)


def mm_t(a, b):
    return jnp.einsum("ka,kc->ac", a, b, precision=high)


def to_rows(block, col_pos, col_count):
    share = block.shape[0] // col_count
    width = block.shape[1]
    out = jnp.zeros((share, width * col_count), block.dtype)
    for m in range(col_count):
        target = col_pos ^ m
        piece = lax.dynamic_slice_in_dim(block, target * share, share, 0)
        if m:
            piece = partner_of(piece, "col", m)
        out = lax.dynamic_update_slice(out, piece, (0, target * width))
    return out


def halves(value):
    top = value.astype(jnp.bfloat16)
    return top, (value - top.astype(jnp.float32)).astype(jnp.bfloat16)


def product(left, right, contract):
    def one(a, b):
        return lax.dot_general(a, b, (contract, ((), ())), preferred_element_type=jnp.float32)

    return one(left[0], right[0]) + (one(left[0], right[1]) + one(left[1], right[0]))


def band_body(count, features, cols, *refs):
    mask_ref, ridge_ref, pos_ref, rows_ref, targets_ref = refs[:5]
    fetched = refs[5 : 5 + count]
    outs = refs[5 + count : 5 + count + cols]
    x_top, x_low, a_top, a_low, squares = refs[5 + count + cols :]
    step = pl.program_id(0)
    share = targets_ref.shape[0]
    flat = ((1,), (1,))

    @pl.when(step == 0)
    def _():
        ones = jnp.ones((8, features), jnp.bfloat16)
        for k in range(count):
            span = pl.ds(k * share, share)
            x = fetched[k][:, :features]
            x_top[span, :], x_low[span, :] = halves(x)
            a_top[span, :], a_low[span, :] = halves(fetched[k][:, features:])
            first, rest = halves(x * x)
            last = (x * x - first.astype(jnp.float32) - rest.astype(jnp.float32)).astype(
                jnp.bfloat16
            )
            total = jnp.zeros((8, share), jnp.float32)
            for part in (last, rest, first):
                total += lax.dot_general(
                    ones, part, (flat, ((), ())), preferred_element_type=jnp.float32
                )
            squares[:, span] = total

    rows = rows_ref[...]
    row_squares = jnp.sum(rows * rows, axis=1, keepdims=True)
    row_halves = halves(rows)
    own = fetched[count // 2][:, features:]
    base = targets_ref[...] - ridge_ref[0] * own
    total = jnp.where(step == pos_ref[0], base, jnp.zeros_like(base))
    for k in range(count):
        span = pl.ds(k * share, share)
        inner = product(row_halves, (x_top[span, :], x_low[span, :]), flat)
        distance = row_squares + squares[0:1, span] - 2.0 * inner
        kernel = jnp.exp(distance * (-2.0 / features))
        kernel = jnp.where(mask_ref[0, k] > 0, kernel, jnp.zeros_like(kernel))
        total -= product(halves(kernel), (a_top[span, :], a_low[span, :]), ((1,), (0,)))
    width = total.shape[1] // cols
    pieces = [total[:, m * width : (m + 1) * width] for m in range(cols)]
    bit = 0
    while 1 << bit < cols:
        odd = (pos_ref[0] >> bit) % 2 == 1
        pieces = [jnp.where(odd, pieces[m ^ (1 << bit)], pieces[m]) for m in range(cols)]
        bit += 1
    for out, piece in zip(outs, pieces):
        out[...] = piece


def band_products(rows_x, fetched, targets, ridge, tile_mask, col_pos, cols):
    leaf_size, features = rows_x.shape
    share, wide = fetched[0].shape
    target_width = targets.shape[1]
    width = target_width // cols
    count = len(fetched)
    smem = pl.BlockSpec(memory_space=pltpu.SMEM)
    whole = lambda shape: pl.BlockSpec(shape, lambda i: (0, 0))
    return pl.pallas_call(
        functools.partial(band_body, count, features, cols),
        grid=(leaf_size // share,),
        in_specs=[smem, smem, smem, pl.BlockSpec((share, features), lambda i: (i, 0))]
        + [whole((share, target_width))]
        + [whole((share, wide))] * count,
        out_specs=[pl.BlockSpec((share, width), lambda i: (i, 0))] * cols,
        out_shape=[jax.ShapeDtypeStruct((leaf_size, width), jnp.float32)] * cols,
        scratch_shapes=[
            pltpu.VMEM((count * share, features), jnp.bfloat16),
            pltpu.VMEM((count * share, features), jnp.bfloat16),
            pltpu.VMEM((count * share, target_width), jnp.bfloat16),
            pltpu.VMEM((count * share, target_width), jnp.bfloat16),
            pltpu.VMEM((8, count * share), jnp.float32),
        ],
        compiler_params=pltpu.CompilerParams(vmem_limit_bytes=40 * 1024 * 1024),
        cost_estimate=pl.CostEstimate(
            flops=12 * leaf_size * share * count * wide // 2,
            bytes_accessed=8 * leaf_size * target_width,
            transcendentals=leaf_size * share * count,
        ),
    )(tile_mask, ridge, jnp.reshape(col_pos, (1,)).astype(jnp.int32), rows_x, targets, *fetched)


def local(
    points,
    coefs,
    targets,
    ridge,
    tile_mask,
    cluster_perm,
    leaf_map,
    leaf_inverse,
    leaf_basis,
    node_inverse,
    node_transfer,
):
    col_count = lax.axis_size("col")
    col_pos = lax.axis_index("col")
    leaf_count = lax.axis_size("leaf")
    leaf_pos = lax.axis_index("leaf")
    share_rows, features = points.shape
    leaf_size = share_rows * col_count
    target_width = coefs.shape[1]
    col_width = target_width // col_count
    band_reach = tile_mask.shape[1] // 2

    packed = jnp.concatenate([points, coefs], axis=1)
    fetched = []
    for offset in range(-band_reach, band_reach + 1):
        fetched.append(shifted(packed, "leaf", -offset) if offset else packed)
    rows_x = jnp.concatenate(exchange(points, "col", col_pos, 0, col_count), axis=0)

    basis = leaf_basis[0]
    solve = leaf_inverse[0]
    rank_size = basis.shape[1]
    order = cluster_perm[0]
    spread = (order[:, None] == jnp.arange(leaf_size, dtype=jnp.int32)[None, :]).astype(jnp.float32)
    up_map = mm(mm_t(basis, solve), spread)

    levels = tree_levels(leaf_count, rank_size)
    shared = []
    for number, (children, low, offset, slice_count) in enumerate(levels):
        node_rows = children * rank_size
        node_inv = node_inverse[0, offset : offset + slice_count, :node_rows]
        own_inv = node_inv
        for fan, digit_low in [level[:2] for level in levels[:number]]:
            own_inv = jnp.concatenate(exchange(own_inv, "leaf", leaf_pos, digit_low, fan), axis=0)
        transfer = None
        lift = None
        if number < len(levels) - 1:
            transfer = node_transfer[0, offset : offset + slice_count]
            whole = transfer
            for fan, digit_low in [level[:2] for level in levels[: number + 1]]:
                whole = jnp.concatenate(exchange(whole, "leaf", leaf_pos, digit_low, fan), axis=0)
            lift = mm(own_inv, whole)
        shared.append((node_inv, own_inv, transfer, lift))

    blocks = list(
        band_products(rows_x, fetched, targets, ridge, tile_mask, col_pos, col_count)
    )
    ready = blocks[-1]
    mask = 1
    while mask < col_count:
        for m in range(col_count - 2 * mask, -1, -2 * mask):
            blocks[m] = blocks[m] + partner_of(blocks[m + mask], "col", mask)
        mask *= 2
    residual = blocks[0]
    late_solve, late_basis, _ = lax.optimization_barrier((solve, basis, ready))
    down_map = mm_t(spread, mm(late_solve, late_basis))

    current = mm(up_map, residual)
    stacks = []
    for number, (children, low, offset, slice_count) in enumerate(levels):
        ordered = exchange(current, "leaf", leaf_pos, low, children)
        if number == 0:
            group_base = leaf_pos // children * children
            slots = lax.dynamic_slice_in_dim(leaf_map, group_base, children, 0) - group_base
            picked = []
            for slot in range(children):
                piece = ordered[0]
                for source in range(1, children):
                    piece = jnp.where(slots[slot] == source, ordered[source], piece)
                picked.append(piece)
            ordered = picked
        stacked = jnp.concatenate(ordered, axis=0)
        stacks.append(stacked)
        if number < len(levels) - 1:
            current = mm_t(shared[number][2], mm(shared[number][0], stacked))
            for fan, digit_low in [level[:2] for level in levels[: number + 1]]:
                current = sum(exchange_raw(current, "leaf", digit_low, fan))
    values = None
    for number in range(len(levels) - 1, -1, -1):
        node_inv, own_inv, transfer, lift = shared[number]
        fresh_values = mm(own_inv, stacks[number])
        values = fresh_values if values is None else fresh_values - mm(lift, values)
    children = levels[0][0]
    local_index = leaf_pos % children
    raw = exchange_raw(values, "leaf", 0, children)
    own_slot = jnp.sum(jnp.arange(children, dtype=jnp.int32) * (slots == local_index))
    incoming = raw[0]
    for m in range(1, children):
        incoming = jnp.where(own_slot == local_index ^ m, raw[m], incoming)

    residual_rows = to_rows(residual, col_pos, col_count)
    solved = mm_t(spread, mm(solve, mm(spread, residual)))
    step = solved - mm(down_map, incoming)
    fresh_rows = coefs + to_rows(step, col_pos, col_count)
    return (residual_rows, fresh_rows)


def solution(mesh):
    return jax.shard_map(
        local,
        mesh=mesh,
        in_specs=(
            P(("leaf", "col"), None),
            P(("leaf", "col"), None),
            P(("leaf", "col"), None),
            P(),
            P("leaf", None),
            P("leaf", None),
            P(),
            P("leaf", None, None),
            P("leaf", None, None),
            P("leaf", None, None),
            P("leaf", None, None),
        ),
        out_specs=(P(("leaf", "col"), None), P(("leaf", "col"), None)),
        check_vma=False,
    )
```
